32 devices in a mesh: out: 4 (over z), con: 4 (over y, core), occ: 2 (over x).
Axes of the slice: x: 2, y: 2, z: 4, core: 2. Of those that a mesh axis runs over, the one named last changes fastest.
Arguments:
- amplitudes: float32 [512, 64, 64], P('con', 'occ', 'out'), may hold values from -6 to 6
- fit_out: float32 [1024, 256], P('con', 'out'), may hold values from -0.12 to 0.12
- fit_con: float32 [1024, 512], P(None, 'con'), may hold values from -0.12 to 0.12
- hole_hole: float32 [64, 64], replicated, may hold values from -0.75 to 0.75
Outputs:
- ladder: float32 [256, 64, 64], P(('out', 'con'), 'occ')
The draws below stay inside these ranges and needn't reach their ends.
All inputs are finite; a program needn't handle non-finite values.
Results may differ from the reference program's by a relative error of at most 0.000075.
Values sent between devices are 32-bit elements; how exact they have to be, the bound alone decides.
A program may use at most 64 MiB of HBM per device.

```python
import jax
import jax.numpy as jnp
from jax import lax

NOCC = 64
NAUX = 1024
NP = 256
NQ = 512


def steps_of(rng, shape, split, smallest, top_value):
    gain = 1.0
    for dim, shards_of in split:
        steps = jax.random.uniform(jax.random.fold_in(jax.random.fold_in(rng, 6), dim), (shards_of,), jnp.float32, smallest / len(split), top_value / len(split))
        gain = gain * jnp.repeat(jnp.exp(steps), shape[dim] // shards_of).reshape((-1,) + (1,) * (len(shape) - 1 - dim))
    return gain


def normal_values(stream_key, extent, spread, bound, pieces=(), kind=jnp.bfloat16):
    result = jax.random.normal(stream_key, extent, jnp.float32) * spread
    if len(pieces) > 0:
        result = steps_of(stream_key, extent, pieces, -0.22, 0.18) * result
    return jnp.clip(result, min=-bound, max=bound).astype(kind)


def setup_inputs(seed: int = 0) -> dict:
    splits = jax.random.split(jax.random.key(seed), 5)
    return {
        "amplitudes": normal_values(splits[0], (NQ, NOCC, NOCC), 1.0, 6.0, ((0, 4), (1, 2), (2, 4)), jnp.float32),
        "fit_out": normal_values(splits[1], (NAUX, NP), 0.02, 0.12, ((0, 4), (1, 4)), jnp.float32),
        "fit_con": normal_values(splits[2], (NAUX, NQ), 0.02, 0.12, ((1, 4),), jnp.float32),
        "hole_hole": normal_values(splits[3], (NOCC, NOCC), NOCC ** -0.5, 0.75, (), jnp.float32),
    }


def reference(amplitudes, fit_out, fit_con, hole_hole):
    highest = lax.Precision.HIGHEST
    dress = jnp.eye(hole_hole.shape[0], dtype=jnp.float32) - hole_hole
    tile = jnp.dot(fit_out.T, fit_con, precision=highest)
    half = jnp.einsum("qim,jm->qij", amplitudes, dress, precision=highest)
    dressed = jnp.einsum("im,qmj->qij", dress, half, precision=highest)
    flat = dressed.reshape(dressed.shape[0], -1)
    ladder = jnp.dot(tile, flat, precision=highest)
    return ladder.reshape(tile.shape[0], dressed.shape[1], dressed.shape[2])
```

```python
import functools

import jax
import jax.numpy as jnp
from jax import lax
from jax.experimental import pallas as pl
from jax.experimental.pallas import tpu as pltpu
from jax.sharding import PartitionSpec as P

highest = lax.Precision.HIGHEST
MESH = pl.DeviceIdType.MESH
LANES = 128
VMEM_BYTES = 40 * 2**20


def split(a):
    hi = a.astype(jnp.bfloat16)
    lo = (a - hi.astype(jnp.float32)).astype(jnp.bfloat16)
    return hi, lo


def product(a, b_hi, b_lo, transposed=False):
    dims = (((1,), (1 if transposed else 0,)), ((), ()))
    dot = functools.partial(lax.dot_general, dimension_numbers=dims, preferred_element_type=jnp.float32)
    hi, lo = split(a)
    rows = a.shape[0]
    both = dot(jnp.concatenate([hi, lo], axis=0), b_hi)
    return both[:rows] + both[rows:] + dot(hi, b_lo)


def flip(index, bits):
    step = 1
    result = index
    while step <= bits:
        if bits & step:
            result = result + step * (1 - 2 * ((index // step) % 2))
        step *= 2
    return result


def kernel(
    sizes, amp_in, out_in, con_in, hole_in, result,
    amps, fit_out, fit_con, hole, dressed, mixer_hi, mixer_lo, tiles, partial, received, summed, last, pieces,
    local_sem, amp_sems, fit_sems, tile_sems, sum_sems, piece_sems,
):
    n_out, n_con, n_occ, own_i, own_n, naux_block, rows = sizes
    rounds = n_con.bit_length() - 1
    lanes = own_i * own_n
    norbs = own_i * n_occ
    group = LANES // own_n
    groups = own_i // group
    z, c, x = lax.axis_index("out"), lax.axis_index("con"), lax.axis_index("occ")

    loads = [
        pltpu.make_async_copy(hole_in, hole, local_sem.at[0]),
        pltpu.make_async_copy(out_in, fit_out.at[c], local_sem.at[1]),
        pltpu.make_async_copy(con_in, fit_con, local_sem.at[2]),
        pltpu.make_async_copy(amp_in, amps.at[x], local_sem.at[3]),
    ]
    for load in loads:
        load.start()

    z_peers = [flip(z, d) for d in range(n_out)]
    c_peers = [flip(c, d) for d in range(n_con)]
    x_peers = [flip(x, d) for d in range(n_occ)]
    barrier = pltpu.get_barrier_semaphore()
    for axis, peers in (("out", z_peers), ("con", c_peers), ("occ", x_peers)):
        for peer in peers[1:]:
            pl.semaphore_signal(barrier, inc=1, device_id={axis: peer}, device_id_type=MESH)
    pl.semaphore_wait(barrier, n_out + n_con + n_occ - 3)

    def send(src, dst, sems, slot, axis, peer):
        copy = pltpu.make_async_remote_copy(
            src_ref=src, dst_ref=dst, send_sem=sems.at[0, slot], recv_sem=sems.at[1, slot],
            device_id={axis: peer}, device_id_type=MESH,
        )
        copy.start()
        return copy

    fit_copies = {
        d: send(out_in, fit_out.at[c], fit_sems, d, "con", c_peers[d]) for d in reversed(range(1, n_con))
    }
    amp_copies = {d: send(amp_in, amps.at[x], amp_sems, d, "occ", x_peers[d]) for d in range(1, n_occ)}

    loads[0].wait()
    eye = (
        lax.broadcasted_iota(jnp.int32, (norbs, norbs), 0) == lax.broadcasted_iota(jnp.int32, (norbs, norbs), 1)
    ).astype(jnp.float32)
    dress = eye - hole[...]
    repeats = LANES // norbs
    turned = jnp.transpose(jnp.concatenate([dress] * repeats, axis=0))
    row_group = lax.broadcasted_iota(jnp.int32, (LANES, LANES), 0) // own_n
    lane_group = lax.broadcasted_iota(jnp.int32, (LANES, LANES), 1) // norbs
    for o in range(n_out):
        block = jnp.concatenate([turned[o * own_n : (o + 1) * own_n]] * group, axis=0)
        for t in range(group // repeats):
            hi, lo = split(jnp.where(row_group == lane_group + t * repeats, block, 0.0))
            at = (slice(o * LANES, (o + 1) * LANES), slice(t * LANES, (t + 1) * LANES))
            mixer_hi[at] = hi
            mixer_lo[at] = lo

    loads[1].wait()
    loads[2].wait()
    tile = None
    for d in range(n_con):
        if d > 0:
            fit_copies[d].wait_recv()
        owner = c_peers[d]
        con_hi, con_lo = split(fit_con[pl.ds(pl.multiple_of(owner * naux_block, naux_block), naux_block), :])
        term = product(fit_out[owner], con_hi, con_lo)
        tile = term if tile is None else tile + term
    tiles[z] = tile
    tile_copies = {
        d: send(tiles.at[z], tiles.at[z], tile_sems, d, "out", z_peers[d]) for d in reversed(range(1, n_out))
    }

    first = pl.multiple_of(x * own_i, own_i)
    own_rows = lax.broadcasted_iota(jnp.int32, (own_i, norbs), 0) + first
    own_eye = (own_rows == lax.broadcasted_iota(jnp.int32, (own_i, norbs), 1)).astype(jnp.float32)
    own_dress = own_eye - hole[pl.ds(first, own_i), :]
    loads[3].wait()
    for d in range(1, n_occ):
        amp_copies[d].wait_recv()
    wide = dressed.shape[1]
    for n in range(0, own_n, 2):
        parts = [
            jnp.concatenate([amps[o, pl.ds(m, own_i, stride=own_n), :] for o in range(n_occ)], axis=0)
            for m in (n, n + 1)
        ]
        hi, lo = split(jnp.concatenate(parts, axis=1))
        value = product(own_dress, hi, lo)
        dressed[pl.ds(n, own_i, stride=own_n), :] = value[:, :wide]
        dressed[pl.ds(n + 1, own_i, stride=own_n), :] = value[:, wide:]
    amp_hi, amp_lo = split(dressed[...])

    sum_copies = {}
    half = n_con // 2
    for d in range(n_out):
        o = z_peers[d]
        if d > 0:
            tile_copies[d].wait_recv()
        value = product(tiles[o], amp_hi, amp_lo, transposed=True)
        partial[o] = value.reshape(half, 2, rows, lanes)
        sum_copies[0, d] = send(
            partial.at[o, :, 1 - c % 2], received.at[o, pl.ds(0, half)], sum_sems, d, "con", c_peers[1]
        )
    piece_copies = {}
    base = 0
    for r in range(rounds):
        count = n_con >> (r + 1)
        for d in range(n_out):
            o = z_peers[d]
            sum_copies[r, d].wait_recv()
            if r == 0:
                total = partial[o, :, c % 2] + received[o, :count]
            else:
                total = summed[o, pl.ds(before + (c // 2**r) % 2, count)] + received[o, base : base + count]
            if r < rounds - 1:
                summed[o, base : base + count] = total
                bit = (c // 2 ** (r + 1)) % 2
                sum_copies[r + 1, d] = send(
                    summed.at[o, pl.ds(base + 1 - bit, count // 2)],
                    received.at[o, pl.ds(base + count, count // 2)],
                    sum_sems, (r + 1) * n_out + d, "con", c_peers[2 ** (r + 1)],
                )
            elif d == 0:
                pieces[o] = total[0]
            else:
                last[o] = total[0]
                piece_copies[d] = send(last.at[o], pieces.at[z], piece_sems, d, "out", o)
        before = base
        base += count

    for d in range(1, n_out):
        piece_copies[d].wait_recv()
    columns = [
        jnp.concatenate([pieces[o, :, g * LANES : (g + 1) * LANES] for g in range(groups)], axis=0)
        for o in range(n_out)
    ]
    final = product(jnp.concatenate(columns, axis=1), mixer_hi[...], mixer_lo[...])
    for t in range(group // repeats):
        lane_tile = final[:, t * LANES : (t + 1) * LANES]
        for s in range(repeats):
            turn = lane_tile if s == 0 else pltpu.roll(lane_tile, LANES - s * norbs, axis=1)
            for g in range(groups):
                i = g * group + t * repeats + s
                result[pl.ds(i, rows, stride=own_i), :] = turn[g * rows : (g + 1) * rows]

    for copies in (fit_copies, amp_copies, tile_copies, sum_copies, piece_copies):
        for copy in copies.values():
            copy.wait_send()


def fused(n_out, n_con, n_occ, amplitudes, fit_out, fit_con, hole_hole):
    pairs, own_i, own_n = amplitudes.shape
    naux_block, own_out = fit_out.shape
    naux = fit_con.shape[0]
    norbs = hole_hole.shape[0]
    rows = own_out // n_con
    lanes = own_i * own_n
    rounds = n_con.bit_length() - 1
    f32, bf16 = jnp.float32, jnp.bfloat16
    wide = (LANES // own_n) * norbs
    dma = pltpu.SemaphoreType.DMA
    result = pl.pallas_call(
        functools.partial(kernel, (n_out, n_con, n_occ, own_i, own_n, naux_block, rows)),
        out_shape=jax.ShapeDtypeStruct((rows * own_i, LANES), f32),
        in_specs=[pl.BlockSpec(memory_space=pl.ANY)] * 4,
        out_specs=pl.BlockSpec(memory_space=pltpu.VMEM),
        scratch_shapes=[
            pltpu.VMEM((n_occ, lanes, pairs), f32),
            pltpu.VMEM((n_con, own_out, naux_block), f32),
            pltpu.VMEM((naux, pairs), f32),
            pltpu.VMEM((norbs, norbs), f32),
            pltpu.VMEM((lanes, pairs), f32),
            pltpu.VMEM((n_out * LANES, wide), bf16),
            pltpu.VMEM((n_out * LANES, wide), bf16),
            pltpu.VMEM((n_out, own_out, pairs), f32),
            pltpu.VMEM((n_out, n_con // 2, 2, rows, lanes), f32),
            pltpu.VMEM((n_out, n_con - 1, rows, lanes), f32),
            pltpu.VMEM((n_out, n_con - 1, rows, lanes), f32),
            pltpu.VMEM((n_out, rows, lanes), f32),
            pltpu.VMEM((n_out, rows, lanes), f32),
            dma((4,)),
            dma((2, n_occ)),
            dma((2, n_con)),
            dma((2, n_out)),
            dma((2, n_out * rounds)),
            dma((2, n_out)),
        ],
        compiler_params=pltpu.CompilerParams(
            collective_id=0, has_side_effects=True, vmem_limit_bytes=VMEM_BYTES
        ),
    )(
        amplitudes.transpose(1, 2, 0).reshape(lanes, pairs),
        fit_out.T,
        fit_con,
        hole_hole,
    )
    return result[:, :norbs].reshape(rows, own_i, norbs)


def unfused(amplitudes, fit_out, fit_con, hole_hole):
    norbs = hole_hole.shape[0]
    dress = jnp.eye(norbs, dtype=jnp.float32) - hole_hole
    tile = jnp.dot(lax.all_gather(fit_out, "con", axis=0, tiled=True).T, fit_con, precision=highest)
    whole = lax.all_gather(amplitudes, "out", axis=2, tiled=True)
    kept_rows = tile.shape[0] // lax.axis_size("con")
    flat = whole.reshape(whole.shape[0], -1)
    total = jnp.dot(tile, flat, precision=highest)
    summed = lax.psum_scatter(
        total.reshape(lax.axis_size("con") * kept_rows, whole.shape[1], whole.shape[2]),
        "con",
        scatter_dimension=0,
        tiled=True,
    )
    right = jnp.einsum("qim,jm->qij", summed, dress, precision=highest)
    complete = lax.all_gather(right, "occ", axis=1, tiled=True)
    own = summed.shape[1]
    first = lax.axis_index("occ") * own
    rows_dress = lax.dynamic_slice_in_dim(dress, first, own, 0)
    return jnp.einsum("im,pmj->pij", rows_dress, complete, precision=highest)


def fits(n_out, n_con, n_occ, amplitudes, fit_out, fit_con, hole_hole):
    pairs, own_i, own_n = amplitudes.shape
    naux_block, own_out = fit_out.shape
    norbs = hole_hole.shape[0]
    lanes = own_i * own_n
    powers = all(n > 1 and n & (n - 1) == 0 for n in (n_out, n_con, n_occ))
    if not powers or own_out % n_con or LANES % own_n or LANES % norbs or own_n % 8 or pairs != LANES:
        return False
    if own_i % (LANES // own_n) or (LANES // own_n) % (LANES // norbs) or own_i % 8:
        return False
    if (own_out // n_con) % 8 or naux_block % LANES or n_con > 4:
        return False
    words = n_out * lanes * (own_out // n_con) * (3 * n_con) + fit_con.size * (3 + n_con * own_out // pairs)
    return 4 * words < VMEM_BYTES // 2


def solution(mesh):
    counts = mesh.shape["out"], mesh.shape["con"], mesh.shape["occ"]

    def local(*arrays):
        if fits(*counts, *arrays):
            return fused(*counts, *arrays)
        return unfused(*arrays)

    placed = (P("con", "occ", "out"), P("con", "out"), P(None, "con"), P())
    return jax.shard_map(
        local, mesh=mesh, in_specs=placed, out_specs=P(("out", "con"), "occ", None), check_vma=False
    )
```

```python
import functools

import jax
import jax.numpy as jnp
from jax import lax
from jax.experimental import pallas as pl
from jax.experimental.pallas import tpu as pltpu
from jax.sharding import PartitionSpec as P

highest = lax.Precision.HIGHEST
MESH = pl.DeviceIdType.MESH
LANES = 128
VMEM_BYTES = 60 * 2**20


def split(a):
    hi = a.astype(jnp.bfloat16)
    lo = (a - hi.astype(jnp.float32)).astype(jnp.bfloat16)
    return hi, lo


def product(a, b_hi, b_lo, transposed=False):
    dims = (((1,), (1 if transposed else 0,)), ((), ()))
    dot = functools.partial(lax.dot_general, dimension_numbers=dims, preferred_element_type=jnp.float32)
    hi, lo = split(a)
    rows = a.shape[0]
    both = dot(jnp.concatenate([hi, lo], axis=0), b_hi)
    return both[:rows] + both[rows:] + dot(hi, b_lo)


def flip(index, bits):
    step = 1
    result = index
    while step <= bits:
        if bits & step:
            result = result + step * (1 - 2 * ((index // step) % 2))
        step *= 2
    return result


def kernel(
    sizes, amp_in, out_in, con_in, hole_in, result,
    amps, fit_out, fit_con, hole, dressed, mixer_hi, mixer_lo, tiles, partial, received, summed, last, pieces,
    local_sem, amp_sems, fit_sems, tile_sems, sum_sems, piece_sems,
):
    n_out, n_con, n_occ, own_i, own_n, naux_block, rows = sizes
    rounds = n_con.bit_length() - 1
    lanes = own_i * own_n
    norbs = own_i * n_occ
    group = LANES // own_n
    groups = own_i // group
    z, c, x = lax.axis_index("out"), lax.axis_index("con"), lax.axis_index("occ")

    loads = [
        pltpu.make_async_copy(hole_in, hole, local_sem.at[0]),
        pltpu.make_async_copy(out_in, fit_out.at[c], local_sem.at[1]),
        pltpu.make_async_copy(con_in, fit_con, local_sem.at[2]),
        pltpu.make_async_copy(amp_in, amps.at[x], local_sem.at[3]),
    ]
    for load in loads:
        load.start()

    z_peers = [flip(z, d) for d in range(n_out)]
    c_peers = [flip(c, d) for d in range(n_con)]
    x_peers = [flip(x, d) for d in range(n_occ)]
    barrier = pltpu.get_barrier_semaphore()
    for axis, peers in (("out", z_peers), ("con", c_peers), ("occ", x_peers)):
        for peer in peers[1:]:
            pl.semaphore_signal(barrier, inc=1, device_id={axis: peer}, device_id_type=MESH)
    pl.semaphore_wait(barrier, n_out + n_con + n_occ - 3)

    def send(src, dst, sems, slot, axis, peer):
        copy = pltpu.make_async_remote_copy(
            src_ref=src, dst_ref=dst, send_sem=sems.at[0, slot], recv_sem=sems.at[1, slot],
            device_id={axis: peer}, device_id_type=MESH,
        )
        copy.start()
        return copy

    fit_copies = {
        d: send(out_in, fit_out.at[c], fit_sems, d, "con", c_peers[d]) for d in reversed(range(1, n_con))
    }
    amp_copies = {d: send(amp_in, amps.at[x], amp_sems, d, "occ", x_peers[d]) for d in range(1, n_occ)}

    loads[0].wait()
    eye = (
        lax.broadcasted_iota(jnp.int32, (norbs, norbs), 0) == lax.broadcasted_iota(jnp.int32, (norbs, norbs), 1)
    ).astype(jnp.float32)
    dress = eye - hole[...]
    repeats = LANES // norbs
    turned = jnp.transpose(jnp.concatenate([dress] * repeats, axis=0))
    row_group = lax.broadcasted_iota(jnp.int32, (LANES, LANES), 0) // own_n
    lane_group = lax.broadcasted_iota(jnp.int32, (LANES, LANES), 1) // norbs
    for o in range(n_out):
        block = jnp.concatenate([turned[o * own_n : (o + 1) * own_n]] * group, axis=0)
        for t in range(group // repeats):
            hi, lo = split(jnp.where(row_group == lane_group + t * repeats, block, 0.0))
            at = (slice(o * LANES, (o + 1) * LANES), slice(t * LANES, (t + 1) * LANES))
            mixer_hi[at] = hi
            mixer_lo[at] = lo

    loads[1].wait()
    loads[2].wait()
    tile = None
    for d in range(n_con):
        if d > 0:
            fit_copies[d].wait_recv()
        owner = c_peers[d]
        con_hi, con_lo = split(fit_con[pl.ds(pl.multiple_of(owner * naux_block, naux_block), naux_block), :])
        term = product(fit_out[owner], con_hi, con_lo)
        tile = term if tile is None else tile + term
    tiles[z] = tile
    tile_copies = {
        d: send(tiles.at[z], tiles.at[z], tile_sems, d, "out", z_peers[d]) for d in reversed(range(1, n_out))
    }

    first = pl.multiple_of(x * own_i, own_i)
    own_rows = lax.broadcasted_iota(jnp.int32, (own_i, norbs), 0) + first
    own_eye = (own_rows == lax.broadcasted_iota(jnp.int32, (own_i, norbs), 1)).astype(jnp.float32)
    own_dress = own_eye - hole[pl.ds(first, own_i), :]
    loads[3].wait()
    for d in range(1, n_occ):
        amp_copies[d].wait_recv()
    wide = dressed.shape[1]
    for n in range(0, own_n, 2):
        parts = [
            jnp.concatenate([amps[o, pl.ds(m, own_i, stride=own_n), :] for o in range(n_occ)], axis=0)
            for m in (n, n + 1)
        ]
        hi, lo = split(jnp.concatenate(parts, axis=1))
        value = product(own_dress, hi, lo)
        dressed[pl.ds(n, own_i, stride=own_n), :] = value[:, :wide]
        dressed[pl.ds(n + 1, own_i, stride=own_n), :] = value[:, wide:]
    amp_hi, amp_lo = split(dressed[...])

    sum_copies = {}
    half = n_con // 2
    for d in range(n_out):
        o = z_peers[d]
        if d > 0:
            tile_copies[d].wait_recv()
        value = product(tiles[o], amp_hi, amp_lo, transposed=True)
        partial[o] = value.reshape(half, 2, rows, lanes)
        sum_copies[0, d] = send(
            partial.at[o, :, 1 - c % 2], received.at[o, pl.ds(0, half)], sum_sems, d, "con", c_peers[1]
        )
    piece_copies = {}
    base = 0
    for r in range(rounds):
        count = n_con >> (r + 1)
        for d in range(n_out):
            o = z_peers[d]
            sum_copies[r, d].wait_recv()
            if r == 0:
                total = partial[o, :, c % 2] + received[o, :count]
            else:
                total = summed[o, pl.ds(before + (c // 2**r) % 2, count)] + received[o, base : base + count]
            if r < rounds - 1:
                summed[o, base : base + count] = total
                bit = (c // 2 ** (r + 1)) % 2
                sum_copies[r + 1, d] = send(
                    summed.at[o, pl.ds(base + 1 - bit, count // 2)],
                    received.at[o, pl.ds(base + count, count // 2)],
                    sum_sems, (r + 1) * n_out + d, "con", c_peers[2 ** (r + 1)],
                )
            elif d == 0:
                pieces[o] = total[0]
            else:
                last[o] = total[0]
                piece_copies[d] = send(last.at[o], pieces.at[z], piece_sems, d, "out", o)
        before = base
        base += count

    for d in range(1, n_out):
        piece_copies[d].wait_recv()
    columns = [
        jnp.concatenate([pieces[o, :, g * LANES : (g + 1) * LANES] for g in range(groups)], axis=0)
        for o in range(n_out)
    ]
    final = product(jnp.concatenate(columns, axis=1), mixer_hi[...], mixer_lo[...])
    for t in range(group // repeats):
        lane_tile = final[:, t * LANES : (t + 1) * LANES]
        for s in range(repeats):
            turn = lane_tile if s == 0 else pltpu.roll(lane_tile, LANES - s * norbs, axis=1)
            for g in range(groups):
                i = g * group + t * repeats + s
                result[pl.ds(i, rows, stride=own_i), :] = turn[g * rows : (g + 1) * rows]

    for copies in (fit_copies, amp_copies, tile_copies, sum_copies, piece_copies):
        for copy in copies.values():
            copy.wait_send()


def fused(n_out, n_con, n_occ, amplitudes, fit_out, fit_con, hole_hole):
    pairs, own_i, own_n = amplitudes.shape
    naux_block, own_out = fit_out.shape
    naux = fit_con.shape[0]
    norbs = hole_hole.shape[0]
    rows = own_out // n_con
    lanes = own_i * own_n
    rounds = n_con.bit_length() - 1
    f32, bf16 = jnp.float32, jnp.bfloat16
    wide = (LANES // own_n) * norbs
    dma = pltpu.SemaphoreType.DMA
    result = pl.pallas_call(
        functools.partial(kernel, (n_out, n_con, n_occ, own_i, own_n, naux_block, rows)),
        out_shape=jax.ShapeDtypeStruct((rows * own_i, LANES), f32),
        in_specs=[pl.BlockSpec(memory_space=pl.ANY)] * 4,
        out_specs=pl.BlockSpec(memory_space=pltpu.VMEM),
        scratch_shapes=[
            pltpu.VMEM((n_occ, lanes, pairs), f32),
            pltpu.VMEM((n_con, own_out, naux_block), f32),
            pltpu.VMEM((naux, pairs), f32),
            pltpu.VMEM((norbs, norbs), f32),
            pltpu.VMEM((lanes, pairs), f32),
            pltpu.VMEM((n_out * LANES, wide), bf16),
            pltpu.VMEM((n_out * LANES, wide), bf16),
            pltpu.VMEM((n_out, own_out, pairs), f32),
            pltpu.VMEM((n_out, n_con // 2, 2, rows, lanes), f32),
            pltpu.VMEM((n_out, n_con - 1, rows, lanes), f32),
            pltpu.VMEM((n_out, n_con - 1, rows, lanes), f32),
            pltpu.VMEM((n_out, rows, lanes), f32),
            pltpu.VMEM((n_out, rows, lanes), f32),
            dma((4,)),
            dma((2, n_occ)),
            dma((2, n_con)),
            dma((2, n_out)),
            dma((2, n_out * rounds)),
            dma((2, n_out)),
        ],
        compiler_params=pltpu.CompilerParams(
            collective_id=0, has_side_effects=True, vmem_limit_bytes=VMEM_BYTES
        ),
    )(
        amplitudes.transpose(1, 2, 0).reshape(lanes, pairs),
        fit_out.T,
        fit_con,
        hole_hole,
    )
    return result[:, :norbs].reshape(rows, own_i, norbs)


def unfused(amplitudes, fit_out, fit_con, hole_hole):
    norbs = hole_hole.shape[0]
    dress = jnp.eye(norbs, dtype=jnp.float32) - hole_hole
    tile = jnp.dot(lax.all_gather(fit_out, "con", axis=0, tiled=True).T, fit_con, precision=highest)
    whole = lax.all_gather(amplitudes, "out", axis=2, tiled=True)
    kept_rows = tile.shape[0] // lax.axis_size("con")
    flat = whole.reshape(whole.shape[0], -1)
    total = jnp.dot(tile, flat, precision=highest)
    summed = lax.psum_scatter(
        total.reshape(lax.axis_size("con") * kept_rows, whole.shape[1], whole.shape[2]),
        "con",
        scatter_dimension=0,
        tiled=True,
    )
    right = jnp.einsum("qim,jm->qij", summed, dress, precision=highest)
    complete = lax.all_gather(right, "occ", axis=1, tiled=True)
    own = summed.shape[1]
    first = lax.axis_index("occ") * own
    rows_dress = lax.dynamic_slice_in_dim(dress, first, own, 0)
    return jnp.einsum("im,pmj->pij", rows_dress, complete, precision=highest)


def fits(n_out, n_con, n_occ, amplitudes, fit_out, fit_con, hole_hole):
    pairs, own_i, own_n = amplitudes.shape
    naux_block, own_out = fit_out.shape
    norbs = hole_hole.shape[0]
    lanes = own_i * own_n
    powers = all(n > 1 and n & (n - 1) == 0 for n in (n_out, n_con, n_occ))
    if not powers or own_out % n_con or LANES % own_n or LANES % norbs or own_n % 8 or pairs != LANES:
        return False
    if own_i % (LANES // own_n) or (LANES // own_n) % (LANES // norbs) or own_i % 8:
        return False
    if (own_out // n_con) % 8 or naux_block % LANES or n_con > 4:
        return False
    words = n_out * lanes * (own_out // n_con) * (3 * n_con) + fit_con.size * (3 + n_con * own_out // pairs)
    return 4 * words < VMEM_BYTES // 2


def solution(mesh):
    counts = mesh.shape["out"], mesh.shape["con"], mesh.shape["occ"]

    def local(*arrays):
        if fits(*counts, *arrays):
            return fused(*counts, *arrays)
        return unfused(*arrays)

    placed = (P("con", "occ", "out"), P("con", "out"), P(None, "con"), P())
    return jax.shard_map(
        local, mesh=mesh, in_specs=placed, out_specs=P(("out", "con"), "occ", None), check_vma=False
    )
```

```python
import functools

import jax
import jax.numpy as jnp
from jax import lax
from jax.experimental import pallas as pl
from jax.experimental.pallas import tpu as pltpu
from jax.sharding import PartitionSpec as P

highest = lax.Precision.HIGHEST
MESH = pl.DeviceIdType.MESH
LANES = 128
VMEM_BYTES = 60 * 2**20


def split(a):
    hi = a.astype(jnp.bfloat16)
    lo = (a - hi.astype(jnp.float32)).astype(jnp.bfloat16)
    return hi, lo


def product(a, b_hi, b_lo, transposed=False):
    dims = (((1,), (1 if transposed else 0,)), ((), ()))
    dot = functools.partial(lax.dot_general, dimension_numbers=dims, preferred_element_type=jnp.float32)
    hi, lo = split(a)
    rows = a.shape[0]
    both = dot(jnp.concatenate([hi, lo], axis=0), b_hi)
    return both[:rows] + both[rows:] + dot(hi, b_lo)


def flip(index, bits):
    step = 1
    result = index
    while step <= bits:
        if bits & step:
            result = result + step * (1 - 2 * ((index // step) % 2))
        step *= 2
    return result


def kernel(
    sizes, amp_in, out_in, con_in, hole_in, result,
    amps, fit_out, fit_con, hole, dressed, mixer_hi, mixer_lo, tiles, partial, received, summed, last, pieces,
    local_sem, amp_sems, fit_sems, tile_sems, sum_sems, piece_sems, news,
):
    n_out, n_con, n_occ, own_i, own_n, naux_block, rows = sizes
    rounds = n_con.bit_length() - 1
    lanes = own_i * own_n
    norbs = own_i * n_occ
    group = LANES // own_n
    groups = own_i // group
    z, c, x = lax.axis_index("out"), lax.axis_index("con"), lax.axis_index("occ")

    loads = [
        pltpu.make_async_copy(hole_in, hole, local_sem.at[0]),
        pltpu.make_async_copy(out_in, fit_out.at[c], local_sem.at[1]),
        pltpu.make_async_copy(con_in, fit_con, local_sem.at[2]),
        pltpu.make_async_copy(amp_in, amps.at[x], local_sem.at[3]),
    ]
    for load in loads:
        load.start()

    z_peers = [flip(z, d) for d in range(n_out)]
    c_peers = [flip(c, d) for d in range(n_con)]
    x_peers = [flip(x, d) for d in range(n_occ)]
    barrier = pltpu.get_barrier_semaphore()
    for axis, peers in (("con", c_peers), ("occ", x_peers)):
        for peer in peers[1:]:
            pl.semaphore_signal(barrier, inc=1, device_id={axis: peer}, device_id_type=MESH)
    for ahead in (1, -1):

        @pl.when((z + ahead >= 0) & (z + ahead < n_out))
        def _():
            pl.semaphore_signal(barrier, inc=1, device_id={"out": z + ahead}, device_id_type=MESH)

    neighbours = jnp.minimum(z, 1) + jnp.minimum(n_out - 1 - z, 1)
    pl.semaphore_wait(barrier, n_con + n_occ - 2 + neighbours)

    def tell(k):
        for ahead in (1, -1):
            about = z - ahead * (k - 1)

            @pl.when((z + ahead >= 0) & (z + ahead < n_out) & (about >= 0) & (about < n_out))
            def _():
                pl.semaphore_signal(
                    news.at[(1 + ahead) // 2, k], inc=1, device_id={"out": z + ahead}, device_id_type=MESH
                )

    def hear(k):
        for ahead in (1, -1):
            about = z - ahead * k

            @pl.when((about >= 0) & (about < n_out))
            def _():
                pl.semaphore_wait(news.at[(1 + ahead) // 2, k], 1)

    def send(src, dst, sems, slot, axis, peer):
        copy = pltpu.make_async_remote_copy(
            src_ref=src, dst_ref=dst, send_sem=sems.at[0, slot], recv_sem=sems.at[1, slot],
            device_id={axis: peer}, device_id_type=MESH,
        )
        copy.start()
        return copy

    fit_copies = {
        d: send(out_in, fit_out.at[c], fit_sems, d, "con", c_peers[d]) for d in reversed(range(1, n_con))
    }
    amp_copies = {d: send(amp_in, amps.at[x], amp_sems, d, "occ", x_peers[d]) for d in range(1, n_occ)}

    if n_out > 2:
        tell(2)

    loads[0].wait()
    eye = (
        lax.broadcasted_iota(jnp.int32, (norbs, norbs), 0) == lax.broadcasted_iota(jnp.int32, (norbs, norbs), 1)
    ).astype(jnp.float32)
    dress = eye - hole[...]
    repeats = LANES // norbs
    turned = jnp.transpose(jnp.concatenate([dress] * repeats, axis=0))
    row_group = lax.broadcasted_iota(jnp.int32, (LANES, LANES), 0) // own_n
    lane_group = lax.broadcasted_iota(jnp.int32, (LANES, LANES), 1) // norbs
    for o in range(n_out):
        block = jnp.concatenate([turned[o * own_n : (o + 1) * own_n]] * group, axis=0)
        for t in range(group // repeats):
            hi, lo = split(jnp.where(row_group == lane_group + t * repeats, block, 0.0))
            at = (slice(o * LANES, (o + 1) * LANES), slice(t * LANES, (t + 1) * LANES))
            mixer_hi[at] = hi
            mixer_lo[at] = lo

    for k in range(2, n_out):
        hear(k)
        if k + 1 < n_out:
            tell(k + 1)

    loads[1].wait()
    loads[2].wait()
    tile = None
    for d in range(n_con):
        if d > 0:
            fit_copies[d].wait_recv()
        owner = c_peers[d]
        con_hi, con_lo = split(fit_con[pl.ds(pl.multiple_of(owner * naux_block, naux_block), naux_block), :])
        term = product(fit_out[owner], con_hi, con_lo)
        tile = term if tile is None else tile + term
    tiles[z] = tile
    tile_copies = {
        d: send(tiles.at[z], tiles.at[z], tile_sems, d, "out", z_peers[d]) for d in reversed(range(1, n_out))
    }

    first = pl.multiple_of(x * own_i, own_i)
    own_rows = lax.broadcasted_iota(jnp.int32, (own_i, norbs), 0) + first
    own_eye = (own_rows == lax.broadcasted_iota(jnp.int32, (own_i, norbs), 1)).astype(jnp.float32)
    own_dress = own_eye - hole[pl.ds(first, own_i), :]
    loads[3].wait()
    for d in range(1, n_occ):
        amp_copies[d].wait_recv()
    wide = dressed.shape[1]
    for n in range(0, own_n, 2):
        parts = [
            jnp.concatenate([amps[o, pl.ds(m, own_i, stride=own_n), :] for o in range(n_occ)], axis=0)
            for m in (n, n + 1)
        ]
        hi, lo = split(jnp.concatenate(parts, axis=1))
        value = product(own_dress, hi, lo)
        dressed[pl.ds(n, own_i, stride=own_n), :] = value[:, :wide]
        dressed[pl.ds(n + 1, own_i, stride=own_n), :] = value[:, wide:]
    amp_hi, amp_lo = split(dressed[...])

    sum_copies, piece_copies = {}, {}
    half = n_con // 2

    def multiply(d):
        o = z_peers[d]
        if d > 0:
            tile_copies[d].wait_recv()
        value = product(tiles[o], amp_hi, amp_lo, transposed=True)
        partial[o] = value.reshape(half, 2, rows, lanes)
        sum_copies[0, d] = send(
            partial.at[o, :, 1 - c % 2], received.at[o, pl.ds(0, half)], sum_sems, d, "con", c_peers[1]
        )

    def fold(r, d):
        o = z_peers[d]
        count = n_con >> (r + 1)
        base = n_con - (n_con >> r)
        sum_copies[r, d].wait_recv()
        if r == 0:
            total = partial[o, :, c % 2] + received[o, :count]
        else:
            before = n_con - (n_con >> (r - 1))
            total = summed[o, pl.ds(before + (c // 2**r) % 2, count)] + received[o, base : base + count]
        if r < rounds - 1:
            summed[o, base : base + count] = total
            bit = (c // 2 ** (r + 1)) % 2
            sum_copies[r + 1, d] = send(
                summed.at[o, pl.ds(base + 1 - bit, count // 2)],
                received.at[o, pl.ds(base + count, count // 2)],
                sum_sems, (r + 1) * n_out + d, "con", c_peers[2 ** (r + 1)],
            )
        elif d == 0:
            pieces[o] = total[0]
        else:
            last[o] = total[0]
            piece_copies[d] = send(last.at[o], pieces.at[z], piece_sems, d, "out", o)

    order = tuple(reversed(range(n_out)))
    for k, d in enumerate(order):
        multiply(d)
        if k > 0:
            fold(0, order[k - 1])
    fold(0, order[-1])
    for r in range(1, rounds):
        for d in reversed(range(n_out)):
            fold(r, d)

    for d in range(1, n_out):
        piece_copies[d].wait_recv()
    columns = [
        jnp.concatenate([pieces[o, :, g * LANES : (g + 1) * LANES] for g in range(groups)], axis=0)
        for o in range(n_out)
    ]
    final = product(jnp.concatenate(columns, axis=1), mixer_hi[...], mixer_lo[...])
    for t in range(group // repeats):
        lane_tile = final[:, t * LANES : (t + 1) * LANES]
        for s in range(repeats):
            turn = lane_tile if s == 0 else pltpu.roll(lane_tile, LANES - s * norbs, axis=1)
            for g in range(groups):
                i = g * group + t * repeats + s
                result[pl.ds(i, rows, stride=own_i), :] = turn[g * rows : (g + 1) * rows]

    for copies in (fit_copies, amp_copies, tile_copies, sum_copies, piece_copies):
        for copy in copies.values():
            copy.wait_send()


def fused(n_out, n_con, n_occ, amplitudes, fit_out, fit_con, hole_hole):
    pairs, own_i, own_n = amplitudes.shape
    naux_block, own_out = fit_out.shape
    naux = fit_con.shape[0]
    norbs = hole_hole.shape[0]
    rows = own_out // n_con
    lanes = own_i * own_n
    rounds = n_con.bit_length() - 1
    f32, bf16 = jnp.float32, jnp.bfloat16
    wide = (LANES // own_n) * norbs
    dma = pltpu.SemaphoreType.DMA
    result = pl.pallas_call(
        functools.partial(kernel, (n_out, n_con, n_occ, own_i, own_n, naux_block, rows)),
        out_shape=jax.ShapeDtypeStruct((rows * own_i, LANES), f32),
        in_specs=[pl.BlockSpec(memory_space=pl.ANY)] * 4,
        out_specs=pl.BlockSpec(memory_space=pltpu.VMEM),
        scratch_shapes=[
            pltpu.VMEM((n_occ, lanes, pairs), f32),
            pltpu.VMEM((n_con, own_out, naux_block), f32),
            pltpu.VMEM((naux, pairs), f32),
            pltpu.VMEM((norbs, norbs), f32),
            pltpu.VMEM((lanes, pairs), f32),
            pltpu.VMEM((n_out * LANES, wide), bf16),
            pltpu.VMEM((n_out * LANES, wide), bf16),
            pltpu.VMEM((n_out, own_out, pairs), f32),
            pltpu.VMEM((n_out, n_con // 2, 2, rows, lanes), f32),
            pltpu.VMEM((n_out, n_con - 1, rows, lanes), f32),
            pltpu.VMEM((n_out, n_con - 1, rows, lanes), f32),
            pltpu.VMEM((n_out, rows, lanes), f32),
            pltpu.VMEM((n_out, rows, lanes), f32),
            dma((4,)),
            dma((2, n_occ)),
            dma((2, n_con)),
            dma((2, n_out)),
            dma((2, n_out * rounds)),
            dma((2, n_out)),
            pltpu.SemaphoreType.REGULAR((2, n_out)),
        ],
        compiler_params=pltpu.CompilerParams(
            collective_id=0, has_side_effects=True, vmem_limit_bytes=VMEM_BYTES
        ),
    )(
        amplitudes.transpose(1, 2, 0).reshape(lanes, pairs),
        fit_out.T,
        fit_con,
        hole_hole,
    )
    return result[:, :norbs].reshape(rows, own_i, norbs)


def unfused(amplitudes, fit_out, fit_con, hole_hole):
    norbs = hole_hole.shape[0]
    dress = jnp.eye(norbs, dtype=jnp.float32) - hole_hole
    tile = jnp.dot(lax.all_gather(fit_out, "con", axis=0, tiled=True).T, fit_con, precision=highest)
    whole = lax.all_gather(amplitudes, "out", axis=2, tiled=True)
    kept_rows = tile.shape[0] // lax.axis_size("con")
    flat = whole.reshape(whole.shape[0], -1)
    total = jnp.dot(tile, flat, precision=highest)
    summed = lax.psum_scatter(
        total.reshape(lax.axis_size("con") * kept_rows, whole.shape[1], whole.shape[2]),
        "con",
        scatter_dimension=0,
        tiled=True,
    )
    right = jnp.einsum("qim,jm->qij", summed, dress, precision=highest)
    complete = lax.all_gather(right, "occ", axis=1, tiled=True)
    own = summed.shape[1]
    first = lax.axis_index("occ") * own
    rows_dress = lax.dynamic_slice_in_dim(dress, first, own, 0)
    return jnp.einsum("im,pmj->pij", rows_dress, complete, precision=highest)


def fits(n_out, n_con, n_occ, amplitudes, fit_out, fit_con, hole_hole):
    pairs, own_i, own_n = amplitudes.shape
    naux_block, own_out = fit_out.shape
    norbs = hole_hole.shape[0]
    lanes = own_i * own_n
    powers = all(n > 1 and n & (n - 1) == 0 for n in (n_out, n_con, n_occ))
    if not powers or own_out % n_con or LANES % own_n or LANES % norbs or own_n % 8 or pairs != LANES:
        return False
    if own_i % (LANES // own_n) or (LANES // own_n) % (LANES // norbs) or own_i % 8:
        return False
    if (own_out // n_con) % 8 or naux_block % LANES or n_con > 4:
        return False
    words = n_out * lanes * (own_out // n_con) * (3 * n_con) + fit_con.size * (3 + n_con * own_out // pairs)
    return 4 * words < VMEM_BYTES // 2


def solution(mesh):
    counts = mesh.shape["out"], mesh.shape["con"], mesh.shape["occ"]

    def local(*arrays):
        if fits(*counts, *arrays):
            return fused(*counts, *arrays)
        return unfused(*arrays)

    placed = (P("con", "occ", "out"), P("con", "out"), P(None, "con"), P())
    return jax.shard_map(
        local, mesh=mesh, in_specs=placed, out_specs=P(("out", "con"), "occ", None), check_vma=False
    )
```
